32 devices in a mesh: groups: 2 (over y), gx: 4 (over z), gy: 2 (over x), gz: 2 (over core).
Axes of the slice: x: 2, y: 2, z: 4, core: 2. Of those that a mesh axis runs over, the one named last changes fastest.
Arguments:
- field: bfloat16 [16, 8, 1024, 512], P('gz', ('groups', 'gx'), 'gy'), parts along dimension 1, may hold values from -6 to 6
- spectral: bfloat16 [1, 32, 32, 16, 1024], P(None, 'gx', 'gy', None, 'gz'), may hold values from -1.5 to 1.5
- pointwise: bfloat16 [1, 16, 16], replicated, may hold values from -1.5 to 1.5
- shift: float32 [1, 16], replicated, may hold values from -3 to 3
Outputs:
- result: bfloat16 [16, 8, 1024, 512], P('gz', ('groups', 'gx'), 'gy'), parts along dimension 1
The draws below stay inside these ranges and needn't reach their ends.
There are 2 independent parts, one for each index of `groups`. The reference program is written for one: setup_inputs(seed, part) draws one part's arguments, and reference() takes and returns one part's arrays. A program takes and returns all parts, laid end to end along the dimension named above; an argument that names none is the same for every part. Nothing has to cross between parts.
All inputs are finite; a program needn't handle non-finite values.
Results may differ from the reference program's by a relative error of at most 0.0069.
Values may be sent and summed in bfloat16 or wider, within the bound.
A program may use at most 128 MiB of HBM per device.

```python
import math
import jax
import jax.numpy as jnp
from jax import lax

CH = 16
KX = 32
KY = 32
KZ = 32
Y = 1024
Z = 512
LAYERS = 1
X = 4


def shard_levels(own_key, shape, cuts, smallest, largest):
    def one(axis_at, blocks):
        draws = jax.random.uniform(jax.random.fold_in(jax.random.fold_in(own_key, 6), axis_at), (blocks,), jnp.float32, smallest / len(cuts), largest / len(cuts))
        return jnp.repeat(jnp.exp(draws), shape[axis_at] // blocks).reshape((-1,) + (1,) * (len(shape) - axis_at - 1))

    loudness = one(*cuts[0])
    for cut in cuts[1:]:
        loudness = loudness * one(*cut)
    return loudness


def noise(stream_key, extent, scale, most, shards=(), kind=jnp.bfloat16):
    values = scale * jax.random.normal(stream_key, extent, jnp.float32)
    if shards:
        values = values * shard_levels(stream_key, extent, shards, -0.22, 0.18)
    return jnp.clip(values, -most, most).astype(kind)


def setup_inputs(seed: int = 0, part: int = 0) -> dict:
    key_list = jax.random.split(jax.random.key(seed), 5)
    own_keys = jax.random.split(jax.random.fold_in(key_list[4], part), 5)
    return {
        "field": noise(own_keys[0], (CH, X, Y, Z), 1.0, 6.0, ((0, 2), (1, 4), (2, 2))),
        "spectral": noise(key_list[1], (LAYERS, KX, KZ, CH, CH * 2 * KY), CH ** -0.5, 1.5, ((1, 4), (2, 2), (4, 2))),
        "pointwise": noise(key_list[2], (LAYERS, CH, CH), CH ** -0.5, 1.5),
        "shift": noise(key_list[3], (LAYERS, CH), 0.5, 3.0, (), jnp.float32),
    }


def phase_table(xs, ys, nx, ny, kx_count, ky_count):
    kx = jnp.arange(kx_count, dtype=jnp.int32) - kx_count // 2
    ky = jnp.arange(ky_count, dtype=jnp.int32) - ky_count // 2
    phase = jnp.mod(kx[None, None, :, None] * xs[:, None, None, None] * ny + ky[None, None, None, :] * ys[None, :, None, None] * nx, nx * ny)
    angle = phase.astype(jnp.float32) * (2.0 * math.pi / (nx * ny))
    return jnp.stack([jnp.cos(angle), jnp.sin(angle)], axis=-1)

def z_tables(zlen, kcount):
    cells = jnp.arange(zlen, dtype=jnp.int32)
    modes = jnp.arange(kcount, dtype=jnp.int32)
    angle = jnp.mod(cells[:, None] * modes[None, :], zlen).astype(jnp.float32) * (2.0 * math.pi / zlen)
    forward = jnp.concatenate([jnp.cos(angle), -jnp.sin(angle)], axis=1)
    weight = jnp.where(modes == 0, 1.0, 2.0).astype(jnp.float32)
    inverse = (forward * jnp.concatenate([weight, weight])[None, :]).T
    return (forward.astype(jnp.bfloat16), inverse.astype(jnp.bfloat16))

def split_parts(prod):
    first = prod[:, 0]
    second = prod[:, 1]
    real = first[..., 0] + second[..., 1]
    imag = second[..., 0] - first[..., 1]
    return jnp.stack([real, imag], axis=1)

def join_parts(prod):
    real = prod[:, 0, ..., 0] - prod[:, 1, ..., 1]
    imag = prod[:, 0, ..., 1] + prod[:, 1, ..., 0]
    return jnp.stack([real, imag], axis=1).transpose(0, 3, 4, 1, 2).astype(jnp.bfloat16)

def mix_modes(spec, weights):
    shaped = weights.astype(jnp.float32).reshape(weights.shape[0], weights.shape[1], CH, CH, 2, KY)
    w_real = shaped[:, :, :, :, 0]
    w_imag = shaped[:, :, :, :, 1]
    s_real = spec[:, :, :, 0].astype(jnp.float32)
    s_imag = spec[:, :, :, 1].astype(jnp.float32)
    m_real = jnp.einsum('abiok,abik->abok', w_real, s_real) - jnp.einsum('abiok,abik->abok', w_imag, s_imag)
    m_imag = jnp.einsum('abiok,abik->abok', w_real, s_imag) + jnp.einsum('abiok,abik->abok', w_imag, s_real)
    return jnp.stack([m_real, m_imag], axis=3).astype(jnp.bfloat16)

def one_layer(field, spectral, pointwise, shift, fz, gz):
    planes = jnp.transpose(field, (1, 0, 2, 3))
    xs = jnp.arange(X, dtype=jnp.int32)
    ys = jnp.arange(Y, dtype=jnp.int32)

    def forward(total, item):
        plane, xpos = item
        zhat = jnp.dot(plane.reshape(CH * Y, Z), fz, preferred_element_type=jnp.float32).astype(jnp.bfloat16).reshape(CH, Y, 2 * KZ)
        table = phase_table(xpos[None], ys, X, Y, KX, KY).astype(jnp.bfloat16).reshape(Y, KX * KY * 2)
        prod = jnp.einsum('cyq,yk->cqk', zhat.astype(jnp.float32), table.astype(jnp.float32))
        return (total + prod, None)
    total, _ = lax.scan(forward, jnp.zeros((CH, 2 * KZ, KX * KY * 2), jnp.float32), (planes, xs))
    parts = split_parts(total.reshape(CH, 2, KZ, KX, KY, 2))
    spec = (parts * (1.0 / math.sqrt(X * Y * Z))).astype(jnp.bfloat16)
    mixed = mix_modes(spec.transpose(3, 2, 0, 1, 4), spectral)
    flat = mixed.transpose(2, 3, 1, 0, 4).reshape(CH * 2 * KZ, KX * KY)
    inverse_scale = 1.0 / math.sqrt(2 * KX * KY * KZ)

    def inverse(carry, item):
        plane, xpos = item
        back = phase_table(xpos[None], ys, X, Y, KX, KY).transpose(2, 3, 0, 1, 4).astype(jnp.bfloat16).reshape(KX * KY, Y * 2)
        prod = jnp.dot(flat, back, preferred_element_type=jnp.float32).reshape(CH, 2, KZ, 1, Y, 2)
        lines = join_parts(prod)
        spectral_out = jnp.dot(lines.reshape(CH * Y, 2 * KZ), gz, preferred_element_type=jnp.float32).reshape(CH, Y, Z) * inverse_scale
        local = jnp.einsum('oi,iyz->oyz', pointwise.astype(jnp.float32), plane.astype(jnp.float32))
        return (carry, jax.nn.gelu(spectral_out + local + shift[:, None, None]).astype(jnp.bfloat16))
    _, outs = lax.scan(inverse, jnp.zeros((), jnp.float32), (planes, xs))
    return outs.transpose(1, 0, 2, 3)

def reference(field, spectral, pointwise, shift):
    fz, gz = z_tables(Z, KZ)
    for layer_index in range(LAYERS):
        field = one_layer(field, spectral[layer_index], pointwise[layer_index], shift[layer_index], fz, gz)
    return field
```

```python
import functools
import math

import jax
import jax.numpy as jnp
import numpy as np
from jax import lax
from jax.experimental import pallas as pl
from jax.experimental.pallas import tpu as pltpu
from jax.sharding import PartitionSpec as P

CH = 16
KX = 32
KY = 32
KZ = 32
LANES = 128
MESH = pl.DeviceIdType.MESH
BF16 = jnp.bfloat16
F32 = jnp.float32


def rows_cols_dot(a, b):
    return lax.dot_general(a, b, (((1,), (1,)), ((), ())), preferred_element_type=F32)


def dot(a, b):
    return jnp.dot(a, b, preferred_element_type=F32)


def as_bf16(table):
    return jnp.asarray(np.asarray(table, np.float32).astype(jnp.bfloat16))


def angles(first, second, period):
    return ((first[:, None] * second[None, :]) % period) * (2.0 * math.pi / period)


def forward_z_table(zlen, count_y):
    angle = angles(np.arange(KZ), np.arange(zlen), zlen).reshape(count_y, -1, zlen)
    return as_bf16(np.stack([np.cos(angle), -np.sin(angle)], axis=1).reshape(2 * KZ, zlen))


def inverse_z_table(zlen):
    angle = angles(np.arange(KZ), np.arange(zlen), zlen)
    weight = np.where(np.arange(KZ) == 0, 1.0, 2.0)[:, None]
    return as_bf16(np.concatenate([weight * np.cos(angle), -weight * np.sin(angle)], axis=1))


def forward_y_table(count_y, rows):
    angle = angles(np.arange(count_y * rows), np.arange(KY) - KY // 2, count_y * rows)
    cosine, sine = np.cos(angle), np.sin(angle)
    parts = [np.concatenate([cosine, -sine], axis=1), np.concatenate([sine, cosine], axis=1)]
    nothing = np.zeros_like(parts[0])
    table = np.stack(
        [
            np.stack([np.concatenate([t, nothing], 1), np.concatenate([nothing, t], 1)])
            for t in parts
        ]
    )
    return as_bf16(table.reshape(2, 2, count_y, rows, LANES).transpose(2, 0, 1, 3, 4))


def inverse_y_table(count_y, rows):
    angle = angles(np.arange(count_y * rows), np.arange(KY) - KY // 2, count_y * rows)
    table = np.concatenate([np.cos(angle), np.sin(angle)], axis=1)
    return as_bf16(table.reshape(count_y, rows, 2 * KY))


def phase_scalars(count_x):
    angle = angles(np.arange(count_x), np.arange(KX) - KX // 2, count_x)
    return jnp.asarray(
        np.concatenate([np.cos(angle).reshape(-1), np.sin(angle).reshape(-1)]).astype(np.float32)
    )


def lane_tables():
    one = np.eye(KY)
    zero = np.zeros((KY, KY))
    half = np.block([[zero, -one], [one, zero]])
    turn = np.kron(np.eye(2), half)
    first = np.block([[one, zero], [zero, -one]])
    second = np.block([[zero, one], [one, zero]])
    wide = np.concatenate([first, first, second, second], axis=1)
    nothing = np.zeros_like(wide)
    spread = np.stack([np.concatenate([wide, nothing], 0), np.concatenate([nothing, wide], 0)])
    return as_bf16(turn), as_bf16(spread)


def row_tables(kz_each):
    table = np.zeros((2, kz_each * CH, 2 * 4 * kz_each))
    for half in range(2):
        for core in range(2):
            for low in range(4):
                for kz in range(kz_each):
                    channel = core * 8 + half * 4 + low
                    table[half, kz * CH + channel, (core * 4 + low) * kz_each + kz] = 1.0
    return as_bf16(table)


def modes_kernel(
    count_x,
    count_y,
    forward_scale,
    field_hbm,
    weights_hbm,
    fz_ref,
    ty_hbm,
    phase_ref,
    turn_ref,
    spread_ref,
    order_ref,
    other_hbm,
    m_ref,
    field_v,
    weights_v,
    ty_v,
    zs,
    sa,
    ra,
    rb,
    s_v,
    p1_v,
    p2_v,
    sc,
    rc,
    field_sem,
    weight_sem,
    ty_sem,
    fs_sem,
    fr_sem,
    as_sem,
    ar_sem,
    bs_sem,
    br_sem,
    cs_sem,
    cr_sem,
):
    mg = lax.axis_index("groups")
    mx = lax.axis_index("gx")
    my = lax.axis_index("gy")
    mz = lax.axis_index("gz")
    channels = field_v.shape[0]
    kz_each = KZ // count_y
    kx_each = KX // count_x
    classes = p1_v.shape[0]
    reps = kx_each // classes

    def device(dx, dy, dz):
        return (
            mg,
            lax.rem(mx + dx, count_x),
            lax.rem(my + dy, count_y),
            lax.rem(mz + dz, 2),
        )

    in_copies = [
        pltpu.make_async_copy(field_hbm.at[c, 0], field_v.at[c], field_sem.at[c])
        for c in range(channels)
    ]
    ty_copy = pltpu.make_async_copy(ty_hbm.at[my], ty_v, ty_sem)
    weight_copy = pltpu.make_async_copy(weights_hbm.at[0], weights_v, weight_sem)
    for copy in in_copies:
        copy.start()
    ty_copy.start()
    weight_copy.start()

    peers = [(0, dy, 0) for dy in range(1, count_y)]
    gather = [(dx, 0, dz) for dx in range(count_x) for dz in range(2) if (dx, dz) != (0, 0)]
    spread = [
        (dx, dy, 0) for dx in range(count_x) for dy in range(count_y) if (dx, dy) != (0, 0)
    ]
    everyone = sorted(set(peers) | set(gather) | set(spread))
    barrier = pltpu.get_barrier_semaphore()
    for offset in everyone:
        pl.semaphore_signal(barrier, inc=1, device_id=device(*offset), device_id_type=MESH)
    pl.semaphore_wait(barrier, len(everyone))

    field_sends = [
        pltpu.make_async_remote_copy(
            src_ref=field_hbm.at[c],
            dst_ref=other_hbm.at[c],
            send_sem=fs_sem.at[c],
            recv_sem=fr_sem.at[c],
            device_id=device(0, 0, 1),
            device_id_type=MESH,
        )
        for c in range(channels)
    ]
    for copy in field_sends:
        copy.start()

    for c in range(channels):
        in_copies[c].wait()
        zhat = rows_cols_dot(fz_ref[...], field_v[c])
        for d in range(count_y):
            for p in range(2):
                row = (d * 2 + p) * kz_each
                zs[d, p, c // 4, pl.ds((c % 4) * kz_each, kz_each), :] = zhat[
                    row : row + kz_each, :
                ]
    ty_copy.wait()
    for d in range(count_y):
        total = None
        for p in range(2):
            for h in range(2):
                term = dot(zs[d, p, h].astype(BF16), ty_v[p, h])
                total = term if total is None else total + term
        sa[d] = total.astype(BF16)

    def a_copy(dy):
        return pltpu.make_async_remote_copy(
            src_ref=sa.at[lax.rem(my + dy, count_y)],
            dst_ref=ra.at[dy],
            send_sem=as_sem.at[dy],
            recv_sem=ar_sem.at[dy],
            device_id=device(0, dy, 0),
            device_id_type=MESH,
        )

    a_copies = [a_copy(dy) for dy in range(1, count_y)]
    for copy in a_copies:
        copy.start()
    total = sa[my].astype(F32)
    for index, copy in enumerate(a_copies):
        copy.wait()
        total = total + ra[index + 1].astype(F32)
    rb[mx, mz] = total.astype(BF16)

    b_copies = [
        pltpu.make_async_remote_copy(
            src_ref=rb.at[mx, mz],
            dst_ref=rb.at[mx, mz],
            send_sem=bs_sem.at[dx, dz],
            recv_sem=br_sem.at[dx, dz],
            device_id=device(dx, 0, dz),
            device_id_type=MESH,
        )
        for dx, _, dz in gather
    ]
    for copy in b_copies:
        copy.start()
    for copy in b_copies:
        copy.wait()

    def phases(x, k):
        at = x * KX + mx * kx_each + k
        return phase_ref[at], phase_ref[count_x * KX + at]

    rows = 2 * 4 * kz_each
    sums = [None] * classes
    for x in range(count_x):
        block = rb[x].reshape(rows, LANES)
        turned = dot(block, turn_ref[...])
        block = block.astype(F32)
        for k in range(classes):
            cosine, sine = phases(x, k)
            term = block * cosine + turned * sine
            sums[k] = term if sums[k] is None else sums[k] + term
    for k in range(classes):
        spec = (sums[k] * forward_scale).astype(BF16)
        wide = dot(order_ref[0], dot(spec, spread_ref[0]).astype(BF16)) + dot(
            order_ref[1], dot(spec, spread_ref[1]).astype(BF16)
        )
        s_v[k] = wide.reshape(kz_each, CH, 2 * LANES)

    weight_copy.wait()
    copies = weights_v.shape[-1] // LANES

    def mix(kz, carry):
        for k in range(classes):
            weight = weights_v[k, kz].astype(F32)
            for r in range(1, reps):
                weight = weight + weights_v[k + r * classes, kz].astype(F32)
            both = s_v[k, kz]
            first = jnp.concatenate([both[:, :LANES]] * copies, axis=1)
            second = jnp.concatenate([both[:, LANES:]] * copies, axis=1)
            p1_v[k, pl.ds(kz, 1), :] = jnp.sum(weight * first, axis=0, keepdims=True)
            p2_v[k, pl.ds(kz, 1), :] = jnp.sum(weight * second, axis=0, keepdims=True)
        return carry

    lax.fori_loop(0, kz_each, mix, 0)

    width = weights_v.shape[-1]
    lane = lax.broadcasted_iota(jnp.int32, (kz_each, width), 1)
    is_real = lax.rem(lane, 2 * KY) < KY
    for x in range(count_x):
        real = imag = None
        for k in range(classes):
            cosine, sine = phases(x, k)
            first, second = p1_v[k], p2_v[k]
            re_term = first * cosine - second * sine
            im_term = second * cosine + first * sine
            real = re_term if real is None else real + re_term
            imag = im_term if imag is None else imag + im_term
        real = real + pltpu.roll(real, width - KY, 1)
        imag = imag + pltpu.roll(imag, KY, 1)
        sc[x] = jnp.where(is_real, real, imag).astype(BF16)

    c_copies = [
        pltpu.make_async_remote_copy(
            src_ref=sc.at[lax.rem(mx + dx, count_x)],
            dst_ref=rc.at[my, mx],
            send_sem=cs_sem.at[dx, dy],
            recv_sem=cr_sem.at[dx, dy],
            device_id=device(dx, dy, 0),
            device_id_type=MESH,
        )
        for dx, dy, _ in spread
    ]
    for copy in c_copies:
        copy.start()
    rc[my, mx] = sc[mx]
    for copy in c_copies:
        copy.wait()
    for d in range(count_y):
        total = rc[d, 0].astype(F32)
        for x in range(1, count_x):
            total = total + rc[d, x].astype(F32)
        m_ref[pl.ds(d * kz_each, kz_each), :] = total
    for copy in field_sends:
        copy.wait()


def modes(field, spectral, count_x, count_y):
    channels, planes, rows, zlen = field.shape
    kx_each, kz_each = spectral.shape[1], spectral.shape[2]
    width = spectral.shape[4]
    classes = count_x if kx_each % count_x == 0 else kx_each
    block = 4 * kz_each
    forward_scale = 1.0 / math.sqrt(count_x * count_y * rows * zlen)
    turn, spread = lane_tables()
    hbm = pl.BlockSpec(memory_space=pl.ANY)
    vmem = pl.BlockSpec(memory_space=pltpu.VMEM)
    smem = pl.BlockSpec(memory_space=pltpu.SMEM)
    dma = pltpu.SemaphoreType.DMA
    return pl.pallas_call(
        functools.partial(modes_kernel, count_x, count_y, forward_scale),
        out_shape=(
            jax.ShapeDtypeStruct(field.shape, BF16),
            jax.ShapeDtypeStruct((KZ, width), F32),
        ),
        in_specs=[hbm, hbm, vmem, hbm, smem, vmem, vmem, vmem],
        out_specs=(hbm, vmem),
        scratch_shapes=[
            pltpu.VMEM((channels, rows, zlen), BF16),
            pltpu.VMEM(spectral.shape[1:], BF16),
            pltpu.VMEM((2, 2, rows, LANES), BF16),
            pltpu.VMEM((count_y, 2, 2, block, rows), F32),
            pltpu.VMEM((count_y, block, LANES), BF16),
            pltpu.VMEM((count_y, block, LANES), BF16),
            pltpu.VMEM((count_x, 2, block, LANES), BF16),
            pltpu.VMEM((classes, kz_each, CH, 2 * LANES), F32),
            pltpu.VMEM((classes, kz_each, width), F32),
            pltpu.VMEM((classes, kz_each, width), F32),
            pltpu.VMEM((count_x, kz_each, width), BF16),
            pltpu.VMEM((count_y, count_x, kz_each, width), BF16),
            dma((channels,)),
            dma,
            dma,
            dma((channels,)),
            dma((channels,)),
            dma((count_y,)),
            dma((count_y,)),
            dma((count_x, 2)),
            dma((count_x, 2)),
            dma((count_x, count_y)),
            dma((count_x, count_y)),
        ],
        compiler_params=pltpu.CompilerParams(
            collective_id=0, has_side_effects=True, vmem_limit_bytes=40 * 1024 * 1024
        ),
        name="modes",
    )(
        field,
        spectral,
        forward_z_table(zlen, count_y),
        forward_y_table(count_y, rows),
        phase_scalars(count_x),
        turn,
        spread,
        row_tables(kz_each),
    )


def cells_kernel(
    inverse_scale, strip, field_ref, other_ref, m_ref, gz_ref, ty_ref, point_ref, shift_ref,
    out_ref, g_v, mix_v,
):
    my = lax.axis_index("gy")
    mz = lax.axis_index("gz")
    channels, _, rows, zlen = field_ref.shape
    step = pl.program_id(0)

    @pl.when(step == 0)
    def _():
        lines = jnp.transpose(m_ref[...]).astype(BF16)
        both = dot(lines, gz_ref[...]) * inverse_scale
        both = both.reshape(channels, 2, KY, 2 * zlen)
        re, im = both[:, 0], both[:, 1]
        g_v[:, :KY, :] = (re[..., :zlen] + im[..., zlen:]).astype(BF16)
        g_v[:, KY:, :] = (re[..., zlen:] - im[..., :zlen]).astype(BF16)

        tall, wide = channels * strip, CH * strip
        pick_row = lax.broadcasted_iota(jnp.int32, (tall, CH), 0) // strip + mz * channels
        left = (pick_row == lax.broadcasted_iota(jnp.int32, (tall, CH), 1)).astype(F32)
        pick_col = lax.rem(
            lax.broadcasted_iota(jnp.int32, (CH, wide), 1) // strip + mz * channels, CH
        )
        right = (pick_col == lax.broadcasted_iota(jnp.int32, (CH, wide), 0)).astype(F32)
        filled = dot(dot(left.astype(BF16), point_ref[0]).astype(BF16), right.astype(BF16))
        at_row = lax.rem(lax.broadcasted_iota(jnp.int32, (tall, wide), 0), strip)
        at_col = lax.rem(lax.broadcasted_iota(jnp.int32, (tall, wide), 1), strip)
        mix_v[...] = jnp.where(at_row == at_col, filled, 0.0).astype(BF16)

    def one_strip(s, carry):
        cells = pl.ds(pl.multiple_of(s * strip, strip), strip)
        own = field_ref[:, 0, cells, :].reshape(channels * strip, zlen)
        other = other_ref[:, 0, cells, :].reshape(channels * strip, zlen)
        local = dot(mix_v[...], jnp.concatenate([own, other], axis=0))
        waves = ty_ref[my, pl.ds(pl.multiple_of(step * rows + s * strip, strip), strip), :]
        for o in range(channels):
            x = dot(waves, g_v[o]) + local[o * strip : (o + 1) * strip]
            x = x + shift_ref[0, mz * channels + o]
            inner = x * (0.7978845608028654 + 0.035677408136300125 * (x * x))
            half = 0.5 * x
            out_ref[o, 0, cells, :] = (half + half * jnp.tanh(inner)).astype(BF16)
        return carry

    lax.fori_loop(0, rows // strip, one_strip, 0)


def cells(field, other, lines, pointwise, shift, count_y):
    channels, planes, rows, zlen = field.shape
    inverse_scale = 1.0 / math.sqrt(2 * KX * KY * KZ)
    tile = min(rows, 64)
    strip = 16
    slab = pl.BlockSpec((channels, 1, tile, zlen), lambda i: (0, 0, i, 0))
    vmem = pl.BlockSpec(memory_space=pltpu.VMEM)
    smem = pl.BlockSpec(memory_space=pltpu.SMEM)
    return pl.pallas_call(
        functools.partial(cells_kernel, inverse_scale, strip),
        grid=(rows // tile,),
        out_shape=jax.ShapeDtypeStruct(field.shape, BF16),
        in_specs=[slab, slab, vmem, vmem, vmem, vmem, smem],
        out_specs=slab,
        scratch_shapes=[
            pltpu.VMEM((channels, 2 * KY, zlen), BF16),
            pltpu.VMEM((channels * strip, CH * strip), BF16),
        ],
        compiler_params=pltpu.CompilerParams(vmem_limit_bytes=40 * 1024 * 1024),
        name="cells",
    )(
        field,
        other,
        lines,
        inverse_z_table(zlen),
        inverse_y_table(count_y, rows),
        pointwise,
        shift,
    )


def on_device(field, spectral, pointwise, shift):
    count_x = lax.axis_size("gx")
    count_y = lax.axis_size("gy")
    for layer in range(spectral.shape[0]):
        other, lines = modes(field, spectral[layer : layer + 1], count_x, count_y)
        field = cells(
            field, other, lines, pointwise[layer : layer + 1], shift[layer : layer + 1], count_y
        )
    return field


def solution(mesh):
    return jax.shard_map(
        on_device,
        mesh=mesh,
        in_specs=(P("gz", ("groups", "gx"), "gy", None), P(None, "gx", "gy", None, "gz"), P(), P()),
        out_specs=P("gz", ("groups", "gx"), "gy", None),
        check_vma=False,
    )
```

```python
import functools
import math

import jax
import jax.numpy as jnp
import numpy as np
from jax import lax
from jax.experimental import pallas as pl
from jax.experimental.pallas import tpu as pltpu
from jax.sharding import PartitionSpec as P

CH = 16
KX = 32
KY = 32
KZ = 32
LANES = 128
VMEM_BYTES = 60 * 1024 * 1024
MESH = pl.DeviceIdType.MESH
BF16 = jnp.bfloat16
F32 = jnp.float32


def rows_cols_dot(a, b):
    return lax.dot_general(a, b, (((1,), (1,)), ((), ())), preferred_element_type=F32)


def dot(a, b):
    return jnp.dot(a, b, preferred_element_type=F32)


def as_bf16(table):
    return np.asarray(table, np.float32).astype(jnp.bfloat16)


def angles(first, second, period):
    return ((first[:, None] * second[None, :]) % period) * (2.0 * math.pi / period)


def forward_z_table(zlen, count_y):
    angle = angles(np.arange(KZ), np.arange(zlen), zlen).reshape(count_y, -1, zlen)
    return as_bf16(np.stack([np.cos(angle), -np.sin(angle)], axis=1).reshape(2 * KZ, zlen))


def inverse_z_table(zlen):
    angle = angles(np.arange(KZ), np.arange(zlen), zlen)
    weight = np.where(np.arange(KZ) == 0, 1.0, 2.0)[:, None]
    return as_bf16(np.concatenate([weight * np.cos(angle), -weight * np.sin(angle)], axis=1))


def forward_y_table(count_y, rows):
    angle = angles(np.arange(count_y * rows), np.arange(KY) - KY // 2, count_y * rows)
    cosine, sine = np.cos(angle), np.sin(angle)
    parts = [np.concatenate([cosine, -sine], axis=1), np.concatenate([sine, cosine], axis=1)]
    nothing = np.zeros_like(parts[0])
    table = np.stack(
        [
            np.stack([np.concatenate([t, nothing], 1), np.concatenate([nothing, t], 1)])
            for t in parts
        ]
    )
    return as_bf16(table.reshape(2, 2, count_y, rows, LANES).transpose(2, 0, 1, 3, 4))


def inverse_y_table(count_y, rows):
    angle = angles(np.arange(count_y * rows), np.arange(KY) - KY // 2, count_y * rows)
    table = np.concatenate([np.cos(angle), np.sin(angle)], axis=1)
    return as_bf16(table.reshape(count_y, rows, 2 * KY))


def phase_rows(count_x):
    angle = angles(np.arange(count_x), np.arange(KX) - KX // 2, count_x)
    both = np.stack([np.cos(angle), np.sin(angle)], axis=-1)
    both = both.reshape(count_x, count_x, -1).transpose(1, 0, 2).reshape(count_x, -1, 1)
    return as_bf16(np.broadcast_to(both, both.shape[:2] + (LANES,)))


def lane_tables():
    one = np.eye(KY)
    zero = np.zeros((KY, KY))
    half = np.block([[zero, -one], [one, zero]])
    turn = np.kron(np.eye(2), half)
    first = np.block([[one, zero], [zero, -one]])
    second = np.block([[zero, one], [one, zero]])
    wide = np.concatenate([first, first, second, second], axis=1)
    nothing = np.zeros_like(wide)
    spread = np.stack([np.concatenate([wide, nothing], 0), np.concatenate([nothing, wide], 0)])
    return as_bf16(turn), as_bf16(spread)


def row_tables(kz_each):
    table = np.zeros((2, kz_each * CH, 2 * 4 * kz_each))
    for half in range(2):
        for core in range(2):
            for low in range(4):
                for kz in range(kz_each):
                    channel = core * 8 + half * 4 + low
                    table[half, kz * CH + channel, (core * 4 + low) * kz_each + kz] = 1.0
    return as_bf16(table)


def in_lanes(table):
    return np.concatenate(np.split(table, table.shape[-1] // LANES, axis=-1), axis=-2)


def modes_kernel(
    count_x,
    count_y,
    forward_scale,
    field_hbm,
    weights_hbm,
    table_hbm,
    point_hbm,
    local_hbm,
    m_ref,
    field_v,
    other_v,
    weights_v,
    ty_v,
    fz_v,
    phase_v,
    turn_v,
    spread_v,
    order_v,
    point_v,
    mix_v,
    local_v,
    zs,
    sa,
    ra,
    rb,
    s_v,
    p1_v,
    p2_v,
    sc,
    rc,
    field_sem,
    weight_sem,
    table_sem,
    local_sem,
    fs_sem,
    fr_sem,
    as_sem,
    ar_sem,
    bs_sem,
    br_sem,
    cs_sem,
    cr_sem,
):
    mg = lax.axis_index("groups")
    mx = lax.axis_index("gx")
    my = lax.axis_index("gy")
    mz = lax.axis_index("gz")
    channels, rows, zlen = field_v.shape
    kz_each = KZ // count_y
    kx_each = KX // count_x
    classes = p1_v.shape[0]
    reps = kx_each // classes

    def device(dx, dy, dz):
        return (
            mg,
            lax.rem(mx + dx, count_x),
            lax.rem(my + dy, count_y),
            lax.rem(mz + dz, 2),
        )

    in_copies = [
        pltpu.make_async_copy(field_hbm.at[c, 0], field_v.at[c], field_sem.at[c])
        for c in range(channels)
    ]
    weight_copy = pltpu.make_async_copy(weights_hbm.at[0], weights_v, weight_sem)
    small = []
    place = 0
    for target, owner, owners in (
        (fz_v, 0, 1),
        (ty_v, my, count_y),
        (turn_v, 0, 1),
        (phase_v, mx, count_x),
        (spread_v, 0, 1),
        (order_v, 0, 1),
    ):
        size = target.shape[0]
        source = table_hbm.at[pl.ds(pl.multiple_of(place + owner * size, 16), size)]
        small.append(pltpu.make_async_copy(source, target, table_sem.at[len(small)]))
        place += owners * size
    small.append(pltpu.make_async_copy(point_hbm.at[0], point_v, table_sem.at[len(small)]))
    fz_copy, ty_copy, *table_copies = small
    fz_copy.start()
    for copy in in_copies:
        copy.start()
    ty_copy.start()
    for copy in table_copies:
        copy.start()
    weight_copy.start()

    peers = [(0, dy, 0) for dy in range(1, count_y)]
    gather = [(dx, 0, dz) for dx in range(count_x) for dz in range(2) if (dx, dz) != (0, 0)]
    spread = [
        (dx, dy, 0) for dx in range(count_x) for dy in range(count_y) if (dx, dy) != (0, 0)
    ]
    everyone = sorted(set(peers) | set(gather) | set(spread))
    barrier = pltpu.get_barrier_semaphore()
    for offset in everyone:
        pl.semaphore_signal(barrier, inc=1, device_id=device(*offset), device_id_type=MESH)

    fz_copy.wait()
    fz = jnp.concatenate(jnp.split(fz_v[...], zlen // LANES, axis=0), axis=1)
    field_sends = [
        pltpu.make_async_remote_copy(
            src_ref=field_hbm.at[c, 0],
            dst_ref=other_v.at[c],
            send_sem=fs_sem.at[c],
            recv_sem=fr_sem.at[c],
            device_id=device(0, 0, 1),
            device_id_type=MESH,
        )
        for c in range(channels)
    ]
    for c in range(channels):
        if c == channels // 2:
            pl.semaphore_wait(barrier, len(everyone))
            for copy in field_sends:
                copy.start()
        in_copies[c].wait()
        zhat = rows_cols_dot(fz, field_v[c])
        for d in range(count_y):
            for p in range(2):
                row = (d * 2 + p) * kz_each
                zs[d, p, c // 4, pl.ds((c % 4) * kz_each, kz_each), :] = zhat[
                    row : row + kz_each, :
                ]
    ty_copy.wait()
    for d in range(count_y):
        total = None
        for p in range(2):
            for h in range(2):
                term = dot(zs[d, p, h].astype(BF16), ty_v[pl.ds((p * 2 + h) * rows, rows), :])
                total = term if total is None else total + term
        sa[d] = total.astype(BF16)

    def a_copy(dy):
        return pltpu.make_async_remote_copy(
            src_ref=sa.at[lax.rem(my + dy, count_y)],
            dst_ref=ra.at[dy],
            send_sem=as_sem.at[dy],
            recv_sem=ar_sem.at[dy],
            device_id=device(0, dy, 0),
            device_id_type=MESH,
        )

    a_copies = [a_copy(dy) for dy in range(1, count_y)]
    for copy in a_copies:
        copy.start()
    total = sa[my].astype(F32)
    for index, copy in enumerate(a_copies):
        copy.wait()
        total = total + ra[index + 1].astype(F32)
    rb[mx, mz] = total.astype(BF16)

    b_copies = [
        pltpu.make_async_remote_copy(
            src_ref=rb.at[mx, mz],
            dst_ref=rb.at[mx, mz],
            send_sem=bs_sem.at[dx, dz],
            recv_sem=br_sem.at[dx, dz],
            device_id=device(dx, 0, dz),
            device_id_type=MESH,
        )
        for dx, _, dz in gather
    ]
    for copy in b_copies:
        copy.start()
    for copy in b_copies:
        copy.wait()

    for copy in table_copies:
        copy.wait()

    phase = phase_v[...].astype(F32)

    def phases(x, k):
        at = 2 * (x * kx_each + k)
        return phase[at : at + 1], phase[at + 1 : at + 2]

    block_rows = 2 * 4 * kz_each
    spread_rows = spread_v.shape[0] // 4
    order_rows = kz_each * CH
    sums = [None] * classes
    for x in range(count_x):
        block = rb[x].reshape(block_rows, LANES)
        turned = dot(block, turn_v[...])
        block = block.astype(F32)
        for k in range(classes):
            cosine, sine = phases(x, k)
            term = block * cosine + turned * sine
            sums[k] = term if sums[k] is None else sums[k] + term
    for k in range(classes):
        spec = (sums[k] * forward_scale).astype(BF16)
        wide = None
        for half in range(2):
            parts = [
                dot(spec, spread_v[pl.ds((half * 2 + t) * spread_rows, spread_rows), :])
                for t in range(2)
            ]
            order = order_v[pl.ds(half * order_rows, order_rows), :block_rows]
            term = dot(order, jnp.concatenate(parts, axis=1).astype(BF16))
            wide = term if wide is None else wide + term
        s_v[k] = wide.reshape(kz_each, CH, 2 * LANES)

    weight_copy.wait()
    copies = weights_v.shape[-1] // LANES

    def mix(kz, carry):
        for k in range(classes):
            weight = weights_v[k, kz].astype(F32)
            for r in range(1, reps):
                weight = weight + weights_v[k + r * classes, kz].astype(F32)
            both = s_v[k, kz]
            first = jnp.concatenate([both[:, :LANES]] * copies, axis=1)
            second = jnp.concatenate([both[:, LANES:]] * copies, axis=1)
            p1_v[k, pl.ds(kz, 1), :] = jnp.sum(weight * first, axis=0, keepdims=True)
            p2_v[k, pl.ds(kz, 1), :] = jnp.sum(weight * second, axis=0, keepdims=True)
        return carry

    lax.fori_loop(0, kz_each, mix, 0)

    width = weights_v.shape[-1]
    lane = lax.broadcasted_iota(jnp.int32, (kz_each, width), 1)
    is_real = lax.rem(lane, 2 * KY) < KY
    for x in range(count_x):
        real = imag = None
        for k in range(classes):
            cosine, sine = (jnp.concatenate([t] * copies, axis=1) for t in phases(x, k))
            first, second = p1_v[k], p2_v[k]
            re_term = first * cosine - second * sine
            im_term = second * cosine + first * sine
            real = re_term if real is None else real + re_term
            imag = im_term if imag is None else imag + im_term
        real = real + pltpu.roll(real, width - KY, 1)
        imag = imag + pltpu.roll(imag, KY, 1)
        sc[x] = jnp.where(is_real, real, imag).astype(BF16)

    c_copies = [
        pltpu.make_async_remote_copy(
            src_ref=sc.at[lax.rem(mx + dx, count_x)],
            dst_ref=rc.at[my, mx],
            send_sem=cs_sem.at[dx, dy],
            recv_sem=cr_sem.at[dx, dy],
            device_id=device(dx, dy, 0),
            device_id_type=MESH,
        )
        for dx, dy, _ in spread
    ]
    for copy in c_copies:
        copy.start()
    rc[my, mx] = sc[mx]

    tall, wide = mix_v.shape
    strip = tall // channels
    pick_row = lax.broadcasted_iota(jnp.int32, (tall, CH), 0) // strip + mz * channels
    left = (pick_row == lax.broadcasted_iota(jnp.int32, (tall, CH), 1)).astype(F32)
    pick_col = lax.rem(
        lax.broadcasted_iota(jnp.int32, (CH, wide), 1) // strip + mz * channels, CH
    )
    right = (pick_col == lax.broadcasted_iota(jnp.int32, (CH, wide), 0)).astype(F32)
    at_row = lax.rem(lax.broadcasted_iota(jnp.int32, (tall, wide), 0), strip)
    at_col = lax.rem(lax.broadcasted_iota(jnp.int32, (tall, wide), 1), strip)
    filled = dot(dot(left.astype(BF16), point_v[...]).astype(BF16), right.astype(BF16))
    mix_v[...] = jnp.where(at_row == at_col, 0.5 * filled, 0.0).astype(BF16)
    for copy in field_sends:
        copy.wait()

    tile = 4 * strip

    def local_copy(i):
        cells = pl.ds(pl.multiple_of(i * tile, tile), tile)
        return pltpu.make_async_copy(
            local_v.at[:, cells, :], local_hbm.at[:, cells, :], local_sem.at[i]
        )

    def pointwise_tile(i, carry):
        for part in range(tile // strip):
            cells = pl.ds(pl.multiple_of(i * tile + part * strip, strip), strip)
            own = field_v[:, cells, :].reshape(channels * strip, zlen)
            other = other_v[:, cells, :].reshape(channels * strip, zlen)
            local = dot(mix_v[...], jnp.concatenate([own, other], axis=0)).astype(BF16)
            local_v[:, cells, :] = local.reshape(channels, strip, zlen)
        local_copy(i).start()
        return carry

    lax.fori_loop(0, rows // tile, pointwise_tile, 0)
    for copy in c_copies:
        copy.wait()
    for d in range(count_y):
        total = rc[d, 0].astype(F32)
        for x in range(1, count_x):
            total = total + rc[d, x].astype(F32)
        m_ref[pl.ds(d * kz_each, kz_each), :] = total
    for i in range(rows // tile):
        local_copy(i).wait()


def modes(field, spectral, pointwise, count_x, count_y):
    channels, planes, rows, zlen = field.shape
    kx_each, kz_each = spectral.shape[1], spectral.shape[2]
    width = spectral.shape[4]
    classes = count_x if kx_each % count_x == 0 else kx_each
    block = 4 * kz_each
    strip = 16
    forward_scale = 1.0 / math.sqrt(count_x * count_y * rows * zlen)
    turn, spread = lane_tables()
    order = row_tables(kz_each)
    order = np.pad(order, ((0, 0), (0, 0), (0, LANES - order.shape[-1])))
    tables = [
        in_lanes(forward_z_table(zlen, count_y)),
        forward_y_table(count_y, rows),
        turn,
        phase_rows(count_x),
        in_lanes(spread),
        order,
    ]
    table = jnp.asarray(np.concatenate([t.reshape(-1, LANES) for t in tables]))
    hbm = pl.BlockSpec(memory_space=pl.ANY)
    vmem = pl.BlockSpec(memory_space=pltpu.VMEM)
    dma = pltpu.SemaphoreType.DMA
    return pl.pallas_call(
        functools.partial(modes_kernel, count_x, count_y, forward_scale),
        out_shape=(
            jax.ShapeDtypeStruct((channels, rows, zlen), BF16),
            jax.ShapeDtypeStruct((KZ, width), F32),
        ),
        in_specs=[hbm, hbm, hbm, hbm],
        out_specs=(hbm, vmem),
        scratch_shapes=[
            pltpu.VMEM((channels, rows, zlen), BF16),
            pltpu.VMEM((channels, rows, zlen), BF16),
            pltpu.VMEM(spectral.shape[1:], BF16),
            pltpu.VMEM((4 * rows, LANES), BF16),
            pltpu.VMEM((2 * KZ * (zlen // LANES), LANES), BF16),
            pltpu.VMEM((count_x * kx_each * 2, LANES), BF16),
            pltpu.VMEM(turn.shape, BF16),
            pltpu.VMEM((4 * LANES, LANES), BF16),
            pltpu.VMEM((2 * kz_each * CH, LANES), BF16),
            pltpu.VMEM(pointwise.shape[1:], BF16),
            pltpu.VMEM((channels * strip, CH * strip), BF16),
            pltpu.VMEM((channels, rows, zlen), BF16),
            pltpu.VMEM((count_y, 2, 2, block, rows), F32),
            pltpu.VMEM((count_y, block, LANES), BF16),
            pltpu.VMEM((count_y, block, LANES), BF16),
            pltpu.VMEM((count_x, 2, block, LANES), BF16),
            pltpu.VMEM((classes, kz_each, CH, 2 * LANES), F32),
            pltpu.VMEM((classes, kz_each, width), F32),
            pltpu.VMEM((classes, kz_each, width), F32),
            pltpu.VMEM((count_x, kz_each, width), BF16),
            pltpu.VMEM((count_y, count_x, kz_each, width), BF16),
            dma((channels,)),
            dma,
            dma((7,)),
            dma((rows // (4 * strip),)),
            dma((channels,)),
            dma((channels,)),
            dma((count_y,)),
            dma((count_y,)),
            dma((count_x, 2)),
            dma((count_x, 2)),
            dma((count_x, count_y)),
            dma((count_x, count_y)),
        ],
        compiler_params=pltpu.CompilerParams(
            collective_id=0, has_side_effects=True, vmem_limit_bytes=VMEM_BYTES
        ),
        name="modes",
    )(field, spectral, table, pointwise)


def cells_kernel(
    inverse_scale, local_hbm, m_hbm, gz_hbm, ty_hbm, shift_ref, out_hbm,
    local_v, m_v, gz_v, ty_v, out_v, g_v, small_sem, local_sem, out_sem,
):
    my = lax.axis_index("gy")
    mz = lax.axis_index("gz")
    channels, rows, zlen = local_v.shape
    part = min(rows, 256)

    small = [
        pltpu.make_async_copy(source, target, small_sem.at[index])
        for index, (source, target) in enumerate(
            [(m_hbm, m_v), (gz_hbm, gz_v), (ty_hbm.at[my], ty_v)]
        )
    ]
    loads = [
        pltpu.make_async_copy(local_hbm.at[o], local_v.at[o], local_sem.at[o])
        for o in range(channels)
    ]
    stores = [
        pltpu.make_async_copy(out_v.at[o], out_hbm.at[o, 0], out_sem.at[o])
        for o in range(channels)
    ]
    for copy in small + loads:
        copy.start()
    for copy in small:
        copy.wait()

    lines = jnp.transpose(m_v[...]).astype(BF16)
    both = dot(lines, gz_v[...]) * (0.5 * inverse_scale)
    both = both.reshape(channels, 2, KY, 2 * zlen)
    re, im = both[:, 0], both[:, 1]
    g_v[:, :KY, :] = (re[..., :zlen] + im[..., zlen:]).astype(BF16)
    g_v[:, KY:, :] = (re[..., zlen:] - im[..., :zlen]).astype(BF16)

    for o in range(channels):
        offset = 0.5 * shift_ref[0, mz * channels + o]
        loads[o].wait()
        for start in range(0, rows, part):
            cells = pl.ds(start, part)
            half = dot(ty_v[cells, :], g_v[o]) + local_v[o, cells, :].astype(F32) + offset
            inner = half * (1.5957691216057308 + 0.285419267290401 * (half * half))
            out_v[o, cells, :] = (half + half * jnp.tanh(inner)).astype(BF16)
        stores[o].start()
    for copy in stores:
        copy.wait()


def cells(local, lines, shift, shape, count_y):
    channels, planes, rows, zlen = shape
    inverse_scale = 1.0 / math.sqrt(2 * KX * KY * KZ)
    hbm = pl.BlockSpec(memory_space=pl.ANY)
    smem = pl.BlockSpec(memory_space=pltpu.SMEM)
    gz_table = inverse_z_table(zlen)
    ty_table = inverse_y_table(count_y, rows)
    dma = pltpu.SemaphoreType.DMA
    return pl.pallas_call(
        functools.partial(cells_kernel, inverse_scale),
        out_shape=jax.ShapeDtypeStruct(shape, BF16),
        in_specs=[hbm, hbm, hbm, hbm, smem],
        out_specs=hbm,
        scratch_shapes=[
            pltpu.VMEM((channels, rows, zlen), BF16),
            pltpu.VMEM(lines.shape, F32),
            pltpu.VMEM(gz_table.shape, BF16),
            pltpu.VMEM(ty_table.shape[1:], BF16),
            pltpu.VMEM((channels, rows, zlen), BF16),
            pltpu.VMEM((channels, 2 * KY, zlen), BF16),
            dma((3,)),
            dma((channels,)),
            dma((channels,)),
        ],
        compiler_params=pltpu.CompilerParams(vmem_limit_bytes=VMEM_BYTES),
        name="cells",
    )(
        local,
        lines,
        jnp.asarray(gz_table),
        jnp.asarray(ty_table),
        shift,
    )


def on_device(field, spectral, pointwise, shift):
    count_x = lax.axis_size("gx")
    count_y = lax.axis_size("gy")
    for layer in range(spectral.shape[0]):
        local, lines = modes(
            field, spectral[layer : layer + 1], pointwise[layer : layer + 1], count_x, count_y
        )
        field = cells(local, lines, shift[layer : layer + 1], field.shape, count_y)
    return field


def solution(mesh):
    return jax.shard_map(
        on_device,
        mesh=mesh,
        in_specs=(P("gz", ("groups", "gx"), "gy", None), P(None, "gx", "gy", None, "gz"), P(), P()),
        out_specs=P("gz", ("groups", "gx"), "gy", None),
        check_vma=False,
    )
```

```python
import functools
import math

import jax
import jax.numpy as jnp
import numpy as np
from jax import lax
from jax.experimental import pallas as pl
from jax.experimental.pallas import tpu as pltpu
from jax.sharding import PartitionSpec as P

CH = 16
KX = 32
KY = 32
KZ = 32
LANES = 128
VMEM_BYTES = 53 * 1024 * 1024
MESH = pl.DeviceIdType.MESH
BF16 = jnp.bfloat16
F32 = jnp.float32


def rows_cols_dot(a, b):
    return lax.dot_general(a, b, (((1,), (1,)), ((), ())), preferred_element_type=F32)


def dot(a, b):
    return jnp.dot(a, b, preferred_element_type=F32)


def as_bf16(table):
    return np.asarray(table, np.float32).astype(jnp.bfloat16)


def angles(first, second, period):
    return ((first[:, None] * second[None, :]) % period) * (2.0 * math.pi / period)


def forward_z_table(zlen, count_y):
    angle = angles(np.arange(KZ), np.arange(zlen), zlen).reshape(count_y, -1, zlen)
    return as_bf16(np.stack([np.cos(angle), -np.sin(angle)], axis=1).reshape(2 * KZ, zlen))


def inverse_z_table(zlen):
    angle = angles(np.arange(KZ), np.arange(zlen), zlen)
    weight = np.where(np.arange(KZ) == 0, 1.0, 2.0)[:, None]
    return as_bf16(np.concatenate([weight * np.cos(angle), -weight * np.sin(angle)], axis=1))


def forward_y_table(count_y, rows):
    angle = angles(np.arange(count_y * rows), np.arange(KY) - KY // 2, count_y * rows)
    cosine, sine = np.cos(angle), np.sin(angle)
    parts = [np.concatenate([cosine, -sine], axis=1), np.concatenate([sine, cosine], axis=1)]
    nothing = np.zeros_like(parts[0])
    table = np.stack(
        [
            np.stack([np.concatenate([t, nothing], 1), np.concatenate([nothing, t], 1)])
            for t in parts
        ]
    )
    return as_bf16(table.reshape(2, 2, count_y, rows, LANES).transpose(2, 0, 1, 3, 4))


def inverse_y_table(count_y, rows):
    angle = angles(np.arange(count_y * rows), np.arange(KY) - KY // 2, count_y * rows)
    table = np.concatenate([np.cos(angle), np.sin(angle)], axis=1)
    return as_bf16(table.reshape(count_y, rows, 2 * KY))


def phase_rows(count_x):
    angle = angles(np.arange(count_x), np.arange(KX) - KX // 2, count_x)
    both = np.stack([np.cos(angle), np.sin(angle)], axis=-1)
    both = both.reshape(count_x, count_x, -1).transpose(1, 0, 2).reshape(count_x, -1, 1)
    return as_bf16(np.broadcast_to(both, both.shape[:2] + (LANES,)))


def lane_tables():
    one = np.eye(KY)
    zero = np.zeros((KY, KY))
    half = np.block([[zero, -one], [one, zero]])
    turn = np.kron(np.eye(2), half)
    first = np.block([[one, zero], [zero, -one]])
    second = np.block([[zero, one], [one, zero]])
    wide = np.concatenate([first, first, second, second], axis=1)
    nothing = np.zeros_like(wide)
    spread = np.stack([np.concatenate([wide, nothing], 0), np.concatenate([nothing, wide], 0)])
    return as_bf16(turn), as_bf16(spread)


def row_tables(kz_each):
    table = np.zeros((2, kz_each * CH, 2 * 4 * kz_each))
    for half in range(2):
        for core in range(2):
            for low in range(4):
                for kz in range(kz_each):
                    channel = core * 8 + half * 4 + low
                    table[half, kz * CH + channel, (core * 4 + low) * kz_each + kz] = 1.0
    return as_bf16(table)


def in_lanes(table):
    return np.concatenate(np.split(table, table.shape[-1] // LANES, axis=-1), axis=-2)


def modes_kernel(
    count_x,
    count_y,
    forward_scale,
    field_hbm,
    weights_hbm,
    table_hbm,
    point_hbm,
    local_hbm,
    m_ref,
    field_v,
    other_v,
    weights_v,
    ty_v,
    fz_v,
    phase_v,
    turn_v,
    spread_v,
    order_v,
    point_v,
    mix_v,
    local_v,
    zs,
    sa,
    ra,
    rb,
    s_v,
    p1_v,
    p2_v,
    sc,
    rc,
    field_sem,
    weight_sem,
    table_sem,
    local_sem,
    fs_sem,
    fr_sem,
    as_sem,
    ar_sem,
    bs_sem,
    br_sem,
    cs_sem,
    cr_sem,
):
    mg = lax.axis_index("groups")
    mx = lax.axis_index("gx")
    my = lax.axis_index("gy")
    mz = lax.axis_index("gz")
    channels, rows, zlen = field_v.shape
    kz_each = KZ // count_y
    kx_each = KX // count_x
    classes = p1_v.shape[0]
    reps = kx_each // classes

    def device(dx, dy, dz):
        return (
            mg,
            lax.rem(mx + dx, count_x),
            lax.rem(my + dy, count_y),
            lax.rem(mz + dz, 2),
        )

    in_copies = [
        pltpu.make_async_copy(field_hbm.at[c, 0], field_v.at[c], field_sem.at[c])
        for c in range(channels)
    ]
    weight_copy = pltpu.make_async_copy(weights_hbm.at[0], weights_v, weight_sem)
    small = []
    place = 0
    for target, owner, owners in (
        (fz_v, 0, 1),
        (ty_v, my, count_y),
        (turn_v, 0, 1),
        (phase_v, mx, count_x),
        (spread_v, 0, 1),
        (order_v, 0, 1),
    ):
        size = target.shape[0]
        source = table_hbm.at[pl.ds(pl.multiple_of(place + owner * size, 16), size)]
        small.append(pltpu.make_async_copy(source, target, table_sem.at[len(small)]))
        place += owners * size
    small.append(pltpu.make_async_copy(point_hbm.at[0], point_v, table_sem.at[len(small)]))
    fz_copy, ty_copy, *table_copies = small
    fz_copy.start()
    for copy in in_copies[:3]:
        copy.start()

    peers = [(0, dy, 0) for dy in range(1, count_y)]
    gather = [(dx, 0, dz) for dx in range(count_x) for dz in range(2) if (dx, dz) != (0, 0)]
    spread = [
        (dx, dy, 0) for dx in range(count_x) for dy in range(count_y) if (dx, dy) != (0, 0)
    ]
    everyone = sorted(set(peers) | set(gather) | set(spread))
    barrier = pltpu.get_barrier_semaphore()
    for offset in everyone:
        pl.semaphore_signal(barrier, inc=1, device_id=device(*offset), device_id_type=MESH)

    fz_copy.wait()
    fz = jnp.concatenate(jnp.split(fz_v[...], zlen // LANES, axis=0), axis=1)
    field_sends = [
        pltpu.make_async_remote_copy(
            src_ref=field_hbm.at[c, 0],
            dst_ref=other_v.at[c],
            send_sem=fs_sem.at[c],
            recv_sem=fr_sem.at[c],
            device_id=device(0, 0, 1),
            device_id_type=MESH,
        )
        for c in range(channels)
    ]
    for c in range(channels):
        in_copies[c].wait()
        if c + 3 < channels:
            in_copies[c + 3].start()
        elif c + 3 == channels:
            ty_copy.start()
        zhat = rows_cols_dot(fz, field_v[c])
        for d in range(count_y):
            for p in range(2):
                row = (d * 2 + p) * kz_each
                zs[d, p, c // 4, pl.ds((c % 4) * kz_each, kz_each), :] = zhat[
                    row : row + kz_each, :
                ]
    for copy in table_copies:
        copy.start()
    weight_copy.start()
    ty_copy.wait()
    for d in range(count_y):
        total = None
        for p in range(2):
            for h in range(2):
                term = dot(zs[d, p, h].astype(BF16), ty_v[pl.ds((p * 2 + h) * rows, rows), :])
                total = term if total is None else total + term
        sa[d] = total.astype(BF16)

    def a_copy(dy):
        return pltpu.make_async_remote_copy(
            src_ref=sa.at[lax.rem(my + dy, count_y)],
            dst_ref=ra.at[dy],
            send_sem=as_sem.at[dy],
            recv_sem=ar_sem.at[dy],
            device_id=device(0, dy, 0),
            device_id_type=MESH,
        )

    a_copies = [a_copy(dy) for dy in range(1, count_y)]
    pl.semaphore_wait(barrier, len(everyone))
    for copy in a_copies:
        copy.start()
    for copy in field_sends:
        copy.start()
    total = sa[my].astype(F32)
    for index, copy in enumerate(a_copies):
        copy.wait()
        total = total + ra[index + 1].astype(F32)
    rb[mx, mz] = total.astype(BF16)

    b_copies = [
        pltpu.make_async_remote_copy(
            src_ref=rb.at[mx, mz],
            dst_ref=rb.at[mx, mz],
            send_sem=bs_sem.at[dx, dz],
            recv_sem=br_sem.at[dx, dz],
            device_id=device(dx, 0, dz),
            device_id_type=MESH,
        )
        for dx, _, dz in gather
    ]
    for copy in b_copies:
        copy.start()
    for copy in b_copies:
        copy.wait()

    for copy in table_copies:
        copy.wait()

    phase = phase_v[...].astype(F32)

    def phases(x, k):
        at = 2 * (x * kx_each + k)
        return phase[at : at + 1], phase[at + 1 : at + 2]

    block_rows = 2 * 4 * kz_each
    spread_rows = spread_v.shape[0] // 4
    order_rows = kz_each * CH
    sums = [None] * classes
    for x in range(count_x):
        block = rb[x].reshape(block_rows, LANES)
        turned = dot(block, turn_v[...])
        block = block.astype(F32)
        for k in range(classes):
            cosine, sine = phases(x, k)
            term = block * cosine + turned * sine
            sums[k] = term if sums[k] is None else sums[k] + term
    for k in range(classes):
        spec = (sums[k] * forward_scale).astype(BF16)
        wide = None
        for half in range(2):
            parts = [
                dot(spec, spread_v[pl.ds((half * 2 + t) * spread_rows, spread_rows), :])
                for t in range(2)
            ]
            order = order_v[pl.ds(half * order_rows, order_rows), :block_rows]
            term = dot(order, jnp.concatenate(parts, axis=1).astype(BF16))
            wide = term if wide is None else wide + term
        s_v[k] = wide.reshape(kz_each, CH, 2 * LANES)

    weight_copy.wait()
    copies = weights_v.shape[-1] // LANES

    def mix(kz, carry):
        for k in range(classes):
            weight = weights_v[k, kz].astype(F32)
            for r in range(1, reps):
                weight = weight + weights_v[k + r * classes, kz].astype(F32)
            both = s_v[k, kz]
            first = jnp.concatenate([both[:, :LANES]] * copies, axis=1)
            second = jnp.concatenate([both[:, LANES:]] * copies, axis=1)
            p1_v[k, pl.ds(kz, 1), :] = jnp.sum(weight * first, axis=0, keepdims=True)
            p2_v[k, pl.ds(kz, 1), :] = jnp.sum(weight * second, axis=0, keepdims=True)
        return carry

    lax.fori_loop(0, kz_each, mix, 0, unroll=4)

    width = weights_v.shape[-1]
    lane = lax.broadcasted_iota(jnp.int32, (kz_each, width), 1)
    is_real = lax.rem(lane, 2 * KY) < KY
    for x in range(count_x):
        real = imag = None
        for k in range(classes):
            cosine, sine = (jnp.concatenate([t] * copies, axis=1) for t in phases(x, k))
            first, second = p1_v[k], p2_v[k]
            re_term = first * cosine - second * sine
            im_term = second * cosine + first * sine
            real = re_term if real is None else real + re_term
            imag = im_term if imag is None else imag + im_term
        real = real + pltpu.roll(real, width - KY, 1)
        imag = imag + pltpu.roll(imag, KY, 1)
        sc[x] = jnp.where(is_real, real, imag).astype(BF16)

    c_copies = [
        pltpu.make_async_remote_copy(
            src_ref=sc.at[lax.rem(mx + dx, count_x)],
            dst_ref=rc.at[my, mx],
            send_sem=cs_sem.at[dx, dy],
            recv_sem=cr_sem.at[dx, dy],
            device_id=device(dx, dy, 0),
            device_id_type=MESH,
        )
        for dx, dy, _ in spread
    ]
    for copy in c_copies:
        copy.start()
    rc[my, mx] = sc[mx]

    tall, wide = mix_v.shape
    strip = tall // channels
    pick_row = lax.broadcasted_iota(jnp.int32, (tall, CH), 0) // strip + mz * channels
    left = (pick_row == lax.broadcasted_iota(jnp.int32, (tall, CH), 1)).astype(F32)
    pick_col = lax.rem(
        lax.broadcasted_iota(jnp.int32, (CH, wide), 1) // strip + mz * channels, CH
    )
    right = (pick_col == lax.broadcasted_iota(jnp.int32, (CH, wide), 0)).astype(F32)
    at_row = lax.rem(lax.broadcasted_iota(jnp.int32, (tall, wide), 0), strip)
    at_col = lax.rem(lax.broadcasted_iota(jnp.int32, (tall, wide), 1), strip)
    filled = dot(dot(left.astype(BF16), point_v[...]).astype(BF16), right.astype(BF16))
    mix_v[...] = jnp.where(at_row == at_col, 0.5 * filled, 0.0).astype(BF16)
    for copy in field_sends:
        copy.wait()

    tile = 4 * strip

    def local_copy(i):
        cells = pl.ds(pl.multiple_of(i * tile, tile), tile)
        return pltpu.make_async_copy(
            local_v.at[:, cells, :], local_hbm.at[:, cells, :], local_sem.at[i]
        )

    def pointwise_tile(i, carry):
        for part in range(tile // strip):
            cells = pl.ds(pl.multiple_of(i * tile + part * strip, strip), strip)
            own = field_v[:, cells, :].reshape(channels * strip, zlen)
            other = other_v[:, cells, :].reshape(channels * strip, zlen)
            local = dot(mix_v[...], jnp.concatenate([own, other], axis=0)).astype(BF16)
            local_v[:, cells, :] = local.reshape(channels, strip, zlen)
        local_copy(i).start()
        return carry

    lax.fori_loop(0, rows // tile, pointwise_tile, 0)
    for copy in c_copies:
        copy.wait()
    for d in range(count_y):
        total = rc[d, 0].astype(F32)
        for x in range(1, count_x):
            total = total + rc[d, x].astype(F32)
        m_ref[pl.ds(d * kz_each, kz_each), :] = total
    for i in range(rows // tile):
        local_copy(i).wait()


def modes(field, spectral, pointwise, count_x, count_y):
    channels, planes, rows, zlen = field.shape
    kx_each, kz_each = spectral.shape[1], spectral.shape[2]
    width = spectral.shape[4]
    classes = count_x if kx_each % count_x == 0 else kx_each
    block = 4 * kz_each
    strip = 16
    forward_scale = 1.0 / math.sqrt(count_x * count_y * rows * zlen)
    turn, spread = lane_tables()
    order = row_tables(kz_each)
    order = np.pad(order, ((0, 0), (0, 0), (0, LANES - order.shape[-1])))
    tables = [
        in_lanes(forward_z_table(zlen, count_y)),
        forward_y_table(count_y, rows),
        turn,
        phase_rows(count_x),
        in_lanes(spread),
        order,
    ]
    table = jnp.asarray(np.concatenate([t.reshape(-1, LANES) for t in tables]))
    hbm = pl.BlockSpec(memory_space=pl.ANY)
    vmem = pl.BlockSpec(memory_space=pltpu.VMEM)
    dma = pltpu.SemaphoreType.DMA
    return pl.pallas_call(
        functools.partial(modes_kernel, count_x, count_y, forward_scale),
        out_shape=(
            jax.ShapeDtypeStruct((channels, rows, zlen), BF16),
            jax.ShapeDtypeStruct((KZ, width), F32),
        ),
        in_specs=[hbm, hbm, hbm, hbm],
        out_specs=(hbm, vmem),
        scratch_shapes=[
            pltpu.VMEM((channels, rows, zlen), BF16),
            pltpu.VMEM((channels, rows, zlen), BF16),
            pltpu.VMEM(spectral.shape[1:], BF16),
            pltpu.VMEM((4 * rows, LANES), BF16),
            pltpu.VMEM((2 * KZ * (zlen // LANES), LANES), BF16),
            pltpu.VMEM((count_x * kx_each * 2, LANES), BF16),
            pltpu.VMEM(turn.shape, BF16),
            pltpu.VMEM((4 * LANES, LANES), BF16),
            pltpu.VMEM((2 * kz_each * CH, LANES), BF16),
            pltpu.VMEM(pointwise.shape[1:], BF16),
            pltpu.VMEM((channels * strip, CH * strip), BF16),
            pltpu.VMEM((channels, rows, zlen), BF16),
            pltpu.VMEM((count_y, 2, 2, block, rows), F32),
            pltpu.VMEM((count_y, block, LANES), BF16),
            pltpu.VMEM((count_y, block, LANES), BF16),
            pltpu.VMEM((count_x, 2, block, LANES), BF16),
            pltpu.VMEM((classes, kz_each, CH, 2 * LANES), F32),
            pltpu.VMEM((classes, kz_each, width), F32),
            pltpu.VMEM((classes, kz_each, width), F32),
            pltpu.VMEM((count_x, kz_each, width), BF16),
            pltpu.VMEM((count_y, count_x, kz_each, width), BF16),
            dma((channels,)),
            dma,
            dma((7,)),
            dma((rows // (4 * strip),)),
            dma((channels,)),
            dma((channels,)),
            dma((count_y,)),
            dma((count_y,)),
            dma((count_x, 2)),
            dma((count_x, 2)),
            dma((count_x, count_y)),
            dma((count_x, count_y)),
        ],
        compiler_params=pltpu.CompilerParams(
            collective_id=0, has_side_effects=True, vmem_limit_bytes=VMEM_BYTES
        ),
        name="modes",
    )(field, spectral, table, pointwise)


def cells_kernel(
    inverse_scale, local_hbm, m_hbm, gz_hbm, ty_hbm, shift_ref, out_hbm,
    local_v, m_v, gz_v, ty_v, out_v, g_v, small_sem, local_sem, out_sem,
):
    my = lax.axis_index("gy")
    mz = lax.axis_index("gz")
    channels, rows, zlen = local_v.shape
    part = min(rows, 256)

    small = [
        pltpu.make_async_copy(source, target, small_sem.at[index])
        for index, (source, target) in enumerate(
            [(m_hbm, m_v), (gz_hbm, gz_v), (ty_hbm.at[my], ty_v)]
        )
    ]
    loads = [
        pltpu.make_async_copy(local_hbm.at[o], local_v.at[o], local_sem.at[o])
        for o in range(channels)
    ]
    parts = rows // part
    stores = [
        pltpu.make_async_copy(
            out_v.at[o, pl.ds(i * part, part), :],
            out_hbm.at[o, 0, pl.ds(i * part, part), :],
            out_sem.at[o * parts + i],
        )
        for o in range(channels)
        for i in range(parts)
    ]
    for copy in small + loads[:2]:
        copy.start()
    for copy in small:
        copy.wait()

    lines = jnp.transpose(m_v[...]).astype(BF16)
    both = dot(lines, gz_v[...]) * (0.5 * inverse_scale)
    both = both.reshape(channels, 2, KY, 2 * zlen)
    re, im = both[:, 0], both[:, 1]
    g_v[:, :KY, :] = (re[..., :zlen] + im[..., zlen:]).astype(BF16)
    g_v[:, KY:, :] = (re[..., zlen:] - im[..., :zlen]).astype(BF16)

    for o in range(channels):
        offset = 0.5 * shift_ref[0, mz * channels + o]
        loads[o].wait()
        if o + 2 < channels:
            loads[o + 2].start()
        for start in range(0, rows, part):
            cells = pl.ds(start, part)
            half = dot(ty_v[cells, :], g_v[o]) + local_v[o, cells, :].astype(F32) + offset
            inner = half * (1.5957691216057308 + 0.285419267290401 * (half * half))
            out_v[o, cells, :] = (half + half * jnp.tanh(inner)).astype(BF16)
            stores[o * parts + start // part].start()
    for copy in stores:
        copy.wait()


def cells(local, lines, shift, shape, count_y):
    channels, planes, rows, zlen = shape
    inverse_scale = 1.0 / math.sqrt(2 * KX * KY * KZ)
    hbm = pl.BlockSpec(memory_space=pl.ANY)
    smem = pl.BlockSpec(memory_space=pltpu.SMEM)
    gz_table = inverse_z_table(zlen)
    ty_table = inverse_y_table(count_y, rows)
    dma = pltpu.SemaphoreType.DMA
    return pl.pallas_call(
        functools.partial(cells_kernel, inverse_scale),
        out_shape=jax.ShapeDtypeStruct(shape, BF16),
        in_specs=[hbm, hbm, hbm, hbm, smem],
        out_specs=hbm,
        scratch_shapes=[
            pltpu.VMEM((channels, rows, zlen), BF16),
            pltpu.VMEM(lines.shape, F32),
            pltpu.VMEM(gz_table.shape, BF16),
            pltpu.VMEM(ty_table.shape[1:], BF16),
            pltpu.VMEM((channels, rows, zlen), BF16),
            pltpu.VMEM((channels, 2 * KY, zlen), BF16),
            dma((3,)),
            dma((channels,)),
            dma((channels * (rows // min(rows, 256)),)),
        ],
        compiler_params=pltpu.CompilerParams(vmem_limit_bytes=VMEM_BYTES),
        name="cells",
    )(
        local,
        lines,
        jnp.asarray(gz_table),
        jnp.asarray(ty_table),
        shift,
    )


def on_device(field, spectral, pointwise, shift):
    count_x = lax.axis_size("gx")
    count_y = lax.axis_size("gy")
    for layer in range(spectral.shape[0]):
        local, lines = modes(
            field, spectral[layer : layer + 1], pointwise[layer : layer + 1], count_x, count_y
        )
        field = cells(local, lines, shift[layer : layer + 1], field.shape, count_y)
    return field


def solution(mesh):
    return jax.shard_map(
        on_device,
        mesh=mesh,
        in_specs=(P("gz", ("groups", "gx"), "gy", None), P(None, "gx", "gy", None, "gz"), P(), P()),
        out_specs=P("gz", ("groups", "gx"), "gy", None),
        check_vma=False,
    )
```
